32 devices in a mesh: dp: 4 (over y, x), expert: 8 (over z, core).
Axes of the slice: x: 2, y: 2, z: 4, core: 2. Of those that a mesh axis runs over, the one named last changes fastest.
Arguments:
- tokens: bfloat16 [4096, 2048], P(('dp', 'expert')), may hold values from -6 to 6
- routes: int32 [4096, 8], P(('dp', 'expert')), may hold values from 0 to 15, all different within a row; in each aligned block of 128 rows (0 to 127, 128 to 255, ...) at most 65 rows name the same one
- route_gates: float32 [4096, 8], P(('dp', 'expert')), may hold values from 0.05 to 0.45
- gate_matrix: bfloat16 [16, 2048, 768], P('expert'), may hold values from -0.125 to 0.125
- up_matrix: bfloat16 [16, 2048, 768], P('expert'), may hold values from -0.125 to 0.125
- down_matrix: bfloat16 [16, 768, 2048], P('expert'), may hold values from -0.21875 to 0.21875
- cotangent: bfloat16 [4096, 2048], P(('dp', 'expert')), may hold values from -6 to 6
Outputs:
- layer_out: bfloat16 [4096, 2048], P(('dp', 'expert'))
- grad_tokens: bfloat16 [4096, 2048], P(('dp', 'expert'))
- grad_gate: bfloat16 [16, 2048, 768], P('expert', 'dp')
- grad_up: bfloat16 [16, 2048, 768], P('expert', 'dp')
- grad_down: bfloat16 [16, 768, 2048], P('expert', None, 'dp')
The draws below stay inside these ranges and needn't reach their ends.
Inputs may be any that keep to these rules, and one draw needn't show every extreme that they name: `routes`: each row names 8 different experts. Among the 128 rows of one device no expert is named more than 65 times, and in every draw some expert is named exactly 65 times by the rows of some device.
All inputs are finite; a program needn't handle non-finite values.
Results may differ from the reference program's by a relative error of at most 0.013.
Values may be sent and summed in bfloat16 or wider, within the bound.
A program may use at most 256 MiB of HBM per device.

```python
import math
import jax
import jax.numpy as jnp
import numpy as np
from jax import lax

D = 2048
FF = 768
TOP = 8
TOK_DEV = 128
EXPERTS = 16
CAP = 65
TOKENS = 4096
N_DP = 4
N_EXPERT = 8


def block_levels(rng, extent, shards, smallest, top_value):
    def one(dim, shards_of):
        heights = jax.random.uniform(jax.random.fold_in(jax.random.fold_in(rng, 6), dim), (shards_of,), jnp.float32, smallest / len(shards), top_value / len(shards))
        return jnp.repeat(jnp.exp(heights), extent[dim] // shards_of).reshape((-1,) + (1,) * (len(extent) - dim - 1))

    gain = one(*shards[0])
    for cut in shards[1:]:
        gain = gain * one(*cut)
    return gain


def shared_out(stream_key, own, number, rows, count, top, most, skew):
    ranking = jax.random.permutation(stream_key, count)
    crowded, ordinary = shares(count, rows * top, most, skew, True), shares(count, rows * top, most, skew, False)
    places = jnp.arange(count)

    def named(tallies, offset_by):
        used = int((tallies > 0).sum())
        fixed = max(1, used // 4)
        moved = fixed + (places - fixed + offset_by * (used - fixed)) % max(1, count - fixed)
        return jnp.zeros((count,), jnp.int32).at[ranking[jnp.where(places < fixed, places, moved)]].set(jnp.asarray(tallies, jnp.int32))

    tallies = jnp.where(number % 4 == 0, named(crowded, number // 4), named(ordinary, number - number // 4 - 1))
    mixed = jax.random.permutation(jax.random.fold_in(own, 3), count)
    donor, taker = mixed[0:count // 2 * 2:2], mixed[1:count // 2 * 2:2]
    room = jnp.minimum(tallies[donor] - 1, most - tallies[taker]) // 2
    room = jnp.where((donor == ranking[0]) | (taker == ranking[0]) | (tallies[taker] == 0), 0, jnp.maximum(room, 0))
    moved = jax.random.randint(jax.random.fold_in(own, 4), (count // 2,), 0, 1 << 20) % (room + 1)
    tallies = tallies.at[donor].add(-moved).at[taker].add(moved)
    members = jnp.searchsorted(jnp.cumsum(tallies), jnp.arange(rows * top), side="right").astype(jnp.int32)
    grid = members.reshape(top, rows).T
    grid = grid[jax.random.permutation(jax.random.fold_in(own, 1), rows)]
    offset_by = jax.random.randint(jax.random.fold_in(own, 2), (rows, 1), 0, top)
    return jnp.take_along_axis(grid, (jnp.arange(top)[None, :] + offset_by) % top, axis=1)


def shares(count, total, reach, skew, full):
    weights = [(1 << 20) // math.isqrt(standing ** skew) + 1 for standing in range(1, count + 1)]
    largest = reach if full else min(reach, max(-(-total // count), total * weights[0] // sum(weights)))
    least = 1 if total - largest >= count - 1 else 0
    counts, surplus = [largest] + [least] * (count - 1), total - largest - least * (count - 1)
    while surplus > 0:
        movable = [i for i in range(1, count) if counts[i] < largest] or [i for i in range(1, count) if counts[i] < reach]
        pool, left = sum([weights[i] for i in movable]), surplus
        for i in movable:
            extra = min(reach - counts[i], max(1, left * weights[i] // pool), surplus)
            counts[i] = counts[i] + extra
            surplus = surplus - extra
    return np.array(counts)


def bell_draw(own_key, shape, deviation, bound, cuts=(), kind=jnp.bfloat16):
    result = deviation * jax.random.normal(own_key, shape, jnp.float32)
    if cuts:
        result = result * block_levels(own_key, shape, cuts, -0.22, 0.18)
    return jnp.clip(result, -bound, bound).astype(kind)


def setup_inputs(seed: int = 0) -> dict:
    keys = jax.random.split(jax.random.key(seed), 8)
    tokens = bell_draw(keys[0], (TOKENS, D), 1.0, 6.0, ((0, 32),))
    routes_keys = jax.random.split(jax.random.fold_in(keys[1], 1), TOKENS // TOK_DEV)
    routes_turns = jax.random.permutation(jax.random.fold_in(keys[1], 3), TOKENS // TOK_DEV)
    routes = jax.vmap(lambda own, number: shared_out(jax.random.fold_in(keys[1], 2), own, number, TOK_DEV, EXPERTS, TOP, CAP, 2))(routes_keys, routes_turns).reshape((TOKENS, TOP))
    route_gates = jnp.clip(0.05 + 0.39999999 * jax.random.uniform(keys[2], (TOKENS, TOP), jnp.float32) ** block_levels(keys[2], (TOKENS, TOP), ((0, 32),), -0.2, 0.2), 0.05, 0.45)
    gate_matrix = bell_draw(keys[3], (EXPERTS, D, FF), D ** -0.5, 0.125, ((0, 8),))
    up_matrix = bell_draw(keys[4], (EXPERTS, D, FF), D ** -0.5, 0.125, ((0, 8),))
    down_matrix = bell_draw(keys[5], (EXPERTS, FF, D), FF ** -0.5, 0.21875, ((0, 8),))
    cotangent = bell_draw(keys[6], (TOKENS, D), 1.0, 6.0, ((0, 32),))
    return {"tokens": tokens, "routes": routes, "route_gates": route_gates, "gate_matrix": gate_matrix, "up_matrix": up_matrix, "down_matrix": down_matrix, "cotangent": cotangent}


def expert_rows(rows_in, scaled, gate_one, up_one, down_one):
    pre_gate = jnp.dot(rows_in, gate_one, preferred_element_type=jnp.float32)
    pre_up = jnp.dot(rows_in, up_one, preferred_element_type=jnp.float32)
    sigmoid_gate = jax.nn.sigmoid(pre_gate)
    activated = pre_gate * sigmoid_gate
    hidden = (activated * pre_up).astype(jnp.bfloat16)
    produced = jnp.dot(hidden, down_one, preferred_element_type=jnp.float32).astype(jnp.bfloat16)
    grad_hidden = jnp.dot(scaled, down_one.T, preferred_element_type=jnp.float32)
    grad_pregate = (grad_hidden * pre_up * sigmoid_gate * (1.0 + pre_gate * (1.0 - sigmoid_gate))).astype(jnp.bfloat16)
    grad_preup = (grad_hidden * activated).astype(jnp.bfloat16)
    returned = (jnp.dot(grad_pregate, gate_one.T, preferred_element_type=jnp.float32)
                + jnp.dot(grad_preup, up_one.T, preferred_element_type=jnp.float32)).astype(jnp.bfloat16)
    part_gate = jnp.dot(rows_in.T, grad_pregate, preferred_element_type=jnp.float32)
    part_up = jnp.dot(rows_in.T, grad_preup, preferred_element_type=jnp.float32)
    part_down = jnp.dot(hidden.T, scaled, preferred_element_type=jnp.float32)
    return produced, returned, part_gate, part_up, part_down


def rounded(value):
    return lax.optimization_barrier(value.astype(jnp.bfloat16)).astype(jnp.float32)


def reference(tokens, routes, route_gates, gate_matrix, up_matrix, down_matrix, cotangent):
    group_tok = TOK_DEV * N_EXPERT
    group_cap = N_EXPERT * CAP

    def one_expert(totals, inputs):
        out_acc, back_acc = totals
        expert, gate_one, up_one, down_one = inputs
        sum_gate = jnp.zeros((D, FF), jnp.float32)
        sum_up = jnp.zeros((D, FF), jnp.float32)
        sum_down = jnp.zeros((FF, D), jnp.float32)
        for group_index in range(N_DP):
            first_row = group_index * group_tok
            flat_ids = routes[first_row:first_row + group_tok].reshape(-1)
            is_hit = flat_ids == expert
            picked = jnp.argsort(jnp.where(is_hit, 0, 1).astype(jnp.int32), stable=True)[:group_cap].astype(jnp.int32)
            is_taken = is_hit[picked]
            token_at = (picked // TOP).astype(jnp.int32)
            gate_at = jnp.where(is_taken, route_gates[first_row:first_row + group_tok].reshape(-1)[picked], 0.0)
            group_tokens = tokens[first_row:first_row + group_tok]
            group_cot = cotangent[first_row:first_row + group_tok]
            rows_in = jnp.where(is_taken[:, None], group_tokens[token_at], jnp.zeros((), jnp.bfloat16))
            scaled = (gate_at[:, None] * group_cot[token_at].astype(jnp.float32)).astype(jnp.bfloat16)
            produced, returned, part_gate, part_up, part_down = expert_rows(rows_in, scaled, gate_one, up_one, down_one)
            target = (first_row + token_at).astype(jnp.int32)
            out_acc = out_acc.at[target].add(gate_at[:, None] * produced.astype(jnp.float32))
            back_acc = back_acc.at[target].add(returned.astype(jnp.float32))
            sum_gate = sum_gate + rounded(part_gate)
            sum_up = sum_up + rounded(part_up)
            sum_down = sum_down + rounded(part_down)
        grads = (sum_gate.astype(jnp.bfloat16), sum_up.astype(jnp.bfloat16), sum_down.astype(jnp.bfloat16))
        return (out_acc, back_acc), grads

    start = (jnp.zeros((TOKENS, D), jnp.float32), jnp.zeros((TOKENS, D), jnp.float32))
    inputs = (jnp.arange(EXPERTS, dtype=jnp.int32), gate_matrix, up_matrix, down_matrix)
    totals, grads = lax.scan(one_expert, start, inputs)
    layer_out = totals[0].astype(jnp.bfloat16)
    grad_tokens = totals[1].astype(jnp.bfloat16)
    return layer_out, grad_tokens, grads[0], grads[1], grads[2]
```

```python
import jax
import jax.numpy as jnp
from jax import lax
from jax.sharding import PartitionSpec as P

F32 = jnp.float32
BF16 = jnp.bfloat16


def dot(a, b, ca, cb):
    return lax.dot_general(a, b, (((ca,), (cb,)), ((), ())), preferred_element_type=F32)


def per_device(tokens, routes, route_gates, gate_matrix, up_matrix, down_matrix, cotangent):
    homes, width, units = gate_matrix.shape
    first = lax.axis_index("expert") * homes
    all_tokens = lax.all_gather(tokens, "expert", axis=0, tiled=True)
    all_cot = lax.all_gather(cotangent, "expert", axis=0, tiled=True)
    all_routes = lax.all_gather(routes, "expert", axis=0, tiled=True)
    all_gates = lax.all_gather(route_gates, "expert", axis=0, tiled=True)

    hidden, grad_pre, grads = [], [], []
    for e in range(homes):
        weight = jnp.sum(jnp.where(all_routes == first + e, all_gates, 0.0), axis=1, keepdims=True)
        picked = jnp.any(all_routes == first + e, axis=1, keepdims=True)
        pre_gate = dot(all_tokens, gate_matrix[e], 1, 0)
        pre_up = dot(all_tokens, up_matrix[e], 1, 0)
        grad_hidden = dot(all_cot, down_matrix[e], 1, 1) * weight
        s = jax.nn.sigmoid(pre_gate)
        act = pre_gate * s
        hidden.append(jnp.where(picked, weight * act * pre_up, 0.0).astype(BF16))
        gpg = (grad_hidden * pre_up * s * (1.0 + pre_gate * (1.0 - s))).astype(BF16)
        gpu = (grad_hidden * act).astype(BF16)
        grad_pre.append((gpg, gpu))
    part_gate = jnp.stack([dot(all_tokens, g[0], 0, 0).astype(BF16) for g in grad_pre])
    part_up = jnp.stack([dot(all_tokens, g[1], 0, 0).astype(BF16) for g in grad_pre])
    part_down = jnp.stack([dot(h, all_cot, 0, 0).astype(BF16) for h in hidden])
    grad_gate = lax.psum_scatter(part_gate, "dp", scatter_dimension=1, tiled=True)
    grad_up = lax.psum_scatter(part_up, "dp", scatter_dimension=1, tiled=True)
    grad_down = lax.psum_scatter(part_down, "dp", scatter_dimension=2, tiled=True)
    out = sum(dot(h, down_matrix[e], 1, 0) for e, h in enumerate(hidden))
    back = sum(
        dot(g[0], gate_matrix[e], 1, 1) + dot(g[1], up_matrix[e], 1, 1)
        for e, g in enumerate(grad_pre)
    )
    layer_out = lax.psum_scatter(out.astype(BF16), "expert", scatter_dimension=0, tiled=True)
    grad_tokens = lax.psum_scatter(back.astype(BF16), "expert", scatter_dimension=0, tiled=True)
    return (layer_out, grad_tokens, grad_gate, grad_up, grad_down)


def solution(mesh):
    row = P(("dp", "expert"), None)
    home = P("expert", None, None)
    return jax.shard_map(
        per_device,
        mesh=mesh,
        in_specs=(row, row, row, home, home, home, row),
        out_specs=(row, row, P("expert", "dp", None), P("expert", "dp", None), P("expert", None, "dp")),
        check_vma=False,
    )
```

```python
import functools

import jax
import jax.numpy as jnp
from jax import lax
from jax.experimental import pallas as pl
from jax.experimental.pallas import tpu as pltpu
from jax.sharding import PartitionSpec as P

F32 = jnp.float32
BF16 = jnp.bfloat16
MIB = 1 << 20


def dot(a, b, ca, cb):
    return lax.dot_general(a, b, (((ca,), (cb,)), ((), ())), preferred_element_type=F32)


def outputs_kernel(homes, *refs):
    gpg, gpu, hid = refs[:homes], refs[homes : 2 * homes], refs[2 * homes : 3 * homes]
    gate, up, down, out, back = refs[3 * homes :]
    acc = dot(hid[0][...], down[0], 1, 0)
    for e in range(1, homes):
        acc += dot(hid[e][...], down[e], 1, 0)
    out[...] = acc.astype(BF16)
    acc = dot(gpg[0][...], gate[0], 1, 1) + dot(gpu[0][...], up[0], 1, 1)
    for e in range(1, homes):
        acc += dot(gpg[e][...], gate[e], 1, 1) + dot(gpu[e][...], up[e], 1, 1)
    back[...] = acc.astype(BF16)


def outputs_call(factors, gate_matrix, up_matrix, down_matrix):
    homes, width, units = gate_matrix.shape
    rows = factors[0].shape[0]
    tile = 256
    whole = pl.BlockSpec((rows, units), lambda i: (0, 0))
    by_row = pl.BlockSpec((homes, tile, units), lambda i: (0, i, 0))
    by_col = pl.BlockSpec((homes, units, tile), lambda i: (0, 0, i))
    flops = 2 * rows * units * width * 3 * homes
    return pl.pallas_call(
        functools.partial(outputs_kernel, homes),
        grid=(width // tile,),
        out_shape=[jax.ShapeDtypeStruct((rows, width), BF16)] * 2,
        in_specs=[whole] * (3 * homes) + [by_row, by_row, by_col],
        out_specs=[pl.BlockSpec((rows, tile), lambda i: (0, i))] * 2,
        compiler_params=pltpu.CompilerParams(vmem_limit_bytes=56 * MIB),
        cost_estimate=pl.CostEstimate(flops=flops, bytes_accessed=36 * MIB, transcendentals=0),
    )(*factors, gate_matrix, up_matrix, down_matrix)


def grads_kernel(count, cols, tok_hbm, cot_hbm, *refs):
    factor_hbm = refs[:count]
    (out, both, factor, turned, stage, relay, land, in_sem, send_sem, relay_sem, land_sem) = refs[count:]
    split = 2 * count // 3
    me = lax.axis_index("dp")
    near_a = me + 1 - 2 * (me % 2)
    near_b = me + 2 - 4 * (me // 2)
    far = 3 - me

    loads = [pltpu.make_async_copy(tok_hbm, both.at[0], in_sem.at[0])]
    loads += [pltpu.make_async_copy(cot_hbm, both.at[1], in_sem.at[1])]
    loads += [
        pltpu.make_async_copy(factor_hbm[j], factor.at[j], in_sem.at[2 + j]) for j in range(count)
    ]
    for load in loads:
        load.start()
    barrier = pltpu.get_barrier_semaphore()
    for peer in (near_a, near_b):
        pl.semaphore_signal(
            barrier, inc=1, device_id={"dp": peer}, device_id_type=pl.DeviceIdType.MESH
        )
    pl.semaphore_wait(barrier, 2)
    for load in loads:
        load.wait()

    def remote(src, dst, send, recv, peer):
        return pltpu.make_async_remote_copy(
            src_ref=src,
            dst_ref=dst,
            send_sem=send,
            recv_sem=recv,
            device_id={"dp": peer},
            device_id_type=pl.DeviceIdType.MESH,
        )

    def to_relay(j, peer):
        return remote(stage.at[0, j], relay.at[j], send_sem.at[0, j], relay_sem.at[j], peer)

    def to_land(way, j, peer):
        return remote(
            stage.at[1 + way, j], land.at[way, j], send_sem.at[1 + way, j], land_sem.at[way, j], peer
        )

    def turn(owner):
        start = pl.multiple_of(owner * cols, cols)
        for side in range(2):
            turned[side] = both[side, :, pl.ds(start, cols)].T

    def chunk(j):
        return dot(turned[j // split], factor[j], 1, 0).astype(BF16)

    pairs = count // 2
    turn(far)

    @pl.loop(0, pairs)
    def _(k):
        for side, peer in ((0, near_a), (1, near_b)):
            j = 2 * k + side
            stage[0, j] = chunk(j)
            to_relay(j, peer).start()

    for way, peer in ((0, near_a), (1, near_b)):
        turn(peer)

        @pl.loop(0, pairs)
        def _(k, way=way, peer=peer):
            j = 2 * k + way
            stage[1 + way, j] = chunk(j)
            to_land(way, j, peer).start()
            other = 2 * k + 1 - way
            stage[1 + way, other] = chunk(other)

    turn(me)

    @pl.loop(0, count)
    def _(j):
        out[j] = chunk(j)

    @pl.loop(0, pairs)
    def _(k):
        for side, peer in ((0, near_a), (1, near_b)):
            j, way = 2 * k + side, 1 - side
            to_relay(j, peer).wait_recv()
            stage[1 + way, j] = (stage[1 + way, j].astype(F32) + relay[j].astype(F32)).astype(BF16)
            to_land(way, j, near_b if way else near_a).start()

    @pl.loop(0, count)
    def _(j):
        to_land(0, j, near_a).wait_recv()
        to_land(1, j, near_b).wait_recv()
        total = out[j].astype(F32) + land[0, j].astype(F32) + land[1, j].astype(F32)
        out[j] = total.astype(BF16)

    @pl.loop(0, count)
    def _(j):
        to_relay(j, near_a).wait_send()
        to_land(0, j, near_a).wait_send()
        to_land(1, j, near_b).wait_send()


def grads_call(all_tokens, all_cot, factors):
    rows, width = all_tokens.shape
    units = factors[0].shape[1]
    count = len(factors)
    cols = width // lax.axis_size("dp")
    piece = (cols, units)
    dma = pltpu.SemaphoreType.DMA
    return pl.pallas_call(
        functools.partial(grads_kernel, count, cols),
        out_shape=jax.ShapeDtypeStruct((count,) + piece, BF16),
        in_specs=[pl.BlockSpec(memory_space=pl.ANY)] * (2 + count),
        out_specs=pl.BlockSpec(memory_space=pltpu.VMEM),
        scratch_shapes=[
            pltpu.VMEM((2, rows, width), BF16),
            pltpu.VMEM((count, rows, units), BF16),
            pltpu.VMEM((2, cols, rows), BF16),
            pltpu.VMEM((3, count) + piece, BF16),
            pltpu.VMEM((count,) + piece, BF16),
            pltpu.VMEM((2, count) + piece, BF16),
            dma((2 + count,)),
            dma((3, count)),
            dma((count,)),
            dma((2, count)),
        ],
        compiler_params=pltpu.CompilerParams(
            collective_id=0, has_side_effects=True, vmem_limit_bytes=60 * MIB
        ),
        cost_estimate=pl.CostEstimate(
            flops=2 * rows * width * units * count * 8, bytes_accessed=24 * MIB, transcendentals=0
        ),
    )(all_tokens, all_cot, *factors)


def per_device(tokens, routes, route_gates, gate_matrix, up_matrix, down_matrix, cotangent):
    homes, width, units = gate_matrix.shape
    first = lax.axis_index("expert") * homes
    all_tokens = lax.all_gather(tokens, "expert", axis=0, tiled=True)
    all_cot = lax.all_gather(cotangent, "expert", axis=0, tiled=True)
    all_routes = lax.all_gather(routes, "expert", axis=0, tiled=True)
    all_gates = lax.all_gather(route_gates, "expert", axis=0, tiled=True)
    rows = all_tokens.shape[0]
    kernels = rows * (2 * width + 3 * homes * units) * 2 <= 18 * MIB and lax.axis_size("dp") == 4

    hidden, gpgs, gpus = [], [], []
    for e in range(homes):
        weight = jnp.sum(jnp.where(all_routes == first + e, all_gates, 0.0), axis=1, keepdims=True)
        pre_gate = dot(all_tokens, gate_matrix[e], 1, 0)
        pre_up = dot(all_tokens, up_matrix[e], 1, 0)
        grad_hidden = dot(all_cot, down_matrix[e], 1, 1) * weight
        s = jax.nn.sigmoid(pre_gate)
        act = pre_gate * s
        hidden.append((weight * act * pre_up).astype(BF16))
        gpgs.append((grad_hidden * pre_up * s * (1.0 + pre_gate * (1.0 - s))).astype(BF16))
        gpus.append((grad_hidden * act).astype(BF16))

    if kernels:
        factors = gpgs + gpus + hidden
        out, back = outputs_call(factors, gate_matrix, up_matrix, down_matrix)
        factors, out, back = lax.optimization_barrier((factors, out, back))
        summed = grads_call(all_tokens, all_cot, factors)
        grad_gate, grad_up = summed[:homes], summed[homes : 2 * homes]
        grad_down = jnp.swapaxes(summed[2 * homes :], 1, 2)
    else:
        part_gate = jnp.stack([dot(all_tokens, g, 0, 0).astype(BF16) for g in gpgs])
        part_up = jnp.stack([dot(all_tokens, g, 0, 0).astype(BF16) for g in gpus])
        part_down = jnp.stack([dot(h, all_cot, 0, 0).astype(BF16) for h in hidden])
        grad_gate = lax.psum_scatter(part_gate, "dp", scatter_dimension=1, tiled=True)
        grad_up = lax.psum_scatter(part_up, "dp", scatter_dimension=1, tiled=True)
        grad_down = lax.psum_scatter(part_down, "dp", scatter_dimension=2, tiled=True)
        out = sum(dot(h, down_matrix[e], 1, 0) for e, h in enumerate(hidden)).astype(BF16)
        back = sum(
            dot(gpgs[e], gate_matrix[e], 1, 1) + dot(gpus[e], up_matrix[e], 1, 1)
            for e in range(homes)
        ).astype(BF16)
    layer_out = lax.psum_scatter(out, "expert", scatter_dimension=0, tiled=True)
    grad_tokens = lax.psum_scatter(back, "expert", scatter_dimension=0, tiled=True)
    return (layer_out, grad_tokens, grad_gate, grad_up, grad_down)


def solution(mesh):
    row = P(("dp", "expert"), None)
    home = P("expert", None, None)
    return jax.shard_map(
        per_device,
        mesh=mesh,
        in_specs=(row, row, row, home, home, home, row),
        out_specs=(row, row, P("expert", "dp", None), P("expert", "dp", None), P("expert", None, "dp")),
        check_vma=False,
    )
```

```python
import functools

import jax
import jax.numpy as jnp
from jax import lax
from jax.experimental import pallas as pl
from jax.experimental.pallas import tpu as pltpu
from jax.sharding import PartitionSpec as P

F32 = jnp.float32
BF16 = jnp.bfloat16
MIB = 1 << 20


def dot(a, b, ca, cb):
    return lax.dot_general(a, b, (((ca,), (cb,)), ((), ())), preferred_element_type=F32)


def gather_kernel(homes, tok, tile, tok_hbm, cot_hbm, mix_hbm, gate_hbm, up_hbm, down_hbm, *refs):
    (xc_out, fac_out, xc, mix, gate, up, down, fac, in_sem, out_sem, line_recv, core_recv) = refs[:12]
    up_send, down_send, core_send = refs[12:]
    units = gate.shape[2]
    tiles = units // tile
    me = lax.axis_index("expert")
    chips = lax.axis_size("expert") // 2
    q, core = me // 2, me % 2
    partner = me + 1 - 2 * core
    first = me * homes

    def rows_of(b, count):
        return pl.ds(pl.multiple_of(b * tok, tok), count * tok)

    own = [
        pltpu.make_async_copy(tok_hbm, xc.at[0, rows_of(me, 1)], in_sem.at[0]),
        pltpu.make_async_copy(cot_hbm, xc.at[1, rows_of(me, 1)], in_sem.at[1]),
        pltpu.make_async_copy(mix_hbm, mix.at[me], in_sem.at[2]),
    ]
    weights = [
        pltpu.make_async_copy(gate_hbm, gate, in_sem.at[3]),
        pltpu.make_async_copy(up_hbm, up, in_sem.at[4]),
        pltpu.make_async_copy(down_hbm, down, in_sem.at[5]),
    ]
    for load in own + weights:
        load.start()

    barrier = pltpu.get_barrier_semaphore()

    def greet(peer):
        pl.semaphore_signal(
            barrier, inc=1, device_id={"expert": peer}, device_id_type=pl.DeviceIdType.MESH
        )

    greet(partner)

    @pl.when(q > 0)
    def _():
        greet(me - 2)

    @pl.when(q < chips - 1)
    def _():
        greet(me + 2)

    pl.semaphore_wait(barrier, jnp.where((q > 0) & (q < chips - 1), 3, 2))
    for load in own:
        load.wait()

    def moves(p, side, send, recv, peer):
        b = 2 * p + side
        return [
            pltpu.make_async_remote_copy(
                src_ref=ref,
                dst_ref=ref,
                send_sem=send.at[kind, p],
                recv_sem=recv.at[kind, p],
                device_id={"expert": peer},
                device_id_type=pl.DeviceIdType.MESH,
            )
            for kind, ref in enumerate((mix.at[b], xc.at[:, rows_of(b, 1), :]))
        ]

    def go_up(p):
        return moves(p, core, up_send, line_recv, me + 2)

    def go_down(p):
        return moves(p, core, down_send, line_recv, me - 2)

    def go_core(p):
        return moves(p, core, core_send, core_recv, partner)

    def start(copies):
        for copy in copies:
            copy.start()

    @pl.when(q < chips - 1)
    def _():
        start(go_up(q))

    @pl.when(q > 0)
    def _():
        start(go_down(q))

    start(go_core(q))
    for load in weights:
        load.wait()

    def stored(p):
        rows = rows_of(2 * p, 2)
        return [
            pltpu.make_async_copy(fac.at[:, rows, :], fac_out.at[:, rows, :], out_sem.at[0, p]),
            pltpu.make_async_copy(xc.at[:, rows, :], xc_out.at[:, rows, :], out_sem.at[1, p]),
        ]

    def compute(p):
        rows = rows_of(2 * p, 2)

        @pl.loop(0, homes * tiles)
        def _(i):
            e = i // tiles
            part = pl.ds(pl.multiple_of((i % tiles) * tile, tile), tile)
            weight = jnp.concatenate(
                [
                    jnp.broadcast_to(mix[2 * p + side, first + e], (128, tok)).T[:, :1]
                    for side in range(2)
                ],
                axis=0,
            )
            pre_gate = dot(xc[0, rows, :], gate[e, :, part], 1, 0)
            pre_up = dot(xc[0, rows, :], up[e, :, part], 1, 0)
            grad_hidden = dot(xc[1, rows, :], down[e, part, :], 1, 1) * weight
            s = jax.nn.sigmoid(pre_gate)
            act = pre_gate * s
            gpg = grad_hidden * pre_up * s * (1.0 + pre_gate * (1.0 - s))
            fac[e, rows, part] = gpg.astype(BF16)
            fac[homes + e, rows, part] = (grad_hidden * act).astype(BF16)
            fac[2 * homes + e, rows, part] = (weight * act * pre_up).astype(BF16)

        start(stored(p))

    @pl.loop(0, chips + 1)
    def _(s):
        below, above = q - s, q + s

        @pl.when((s > 0) & (below >= 0))
        def _():
            for copy in moves(below, core, up_send, line_recv, me - 2):
                copy.wait_recv()

            @pl.when(q < chips - 1)
            def _():
                start(go_up(below))

            start(go_core(below))

        @pl.when((s > 0) & (above < chips))
        def _():
            for copy in moves(above, core, down_send, line_recv, me + 2):
                copy.wait_recv()

            @pl.when(q > 0)
            def _():
                start(go_down(above))

            start(go_core(above))

        @pl.loop(0, 2)
        def _(side):
            p = q + (2 * side - 1) * (s - 1)

            @pl.when((s > side) & (p >= 0) & (p < chips))
            def _():
                for copy in moves(p, 1 - core, core_send, core_recv, partner):
                    copy.wait_recv()
                compute(p)

    @pl.loop(0, chips)
    def _(p):
        for copy in stored(p):
            copy.wait()
        for copy in go_core(p):
            copy.wait_send()

        @pl.when((p <= q) & (q < chips - 1))
        def _():
            for copy in go_up(p):
                copy.wait_send()

        @pl.when((p >= q) & (q > 0))
        def _():
            for copy in go_down(p):
                copy.wait_send()


def gather_call(tokens, cotangent, mix, gate_matrix, up_matrix, down_matrix):
    homes, width, units = gate_matrix.shape
    tok = tokens.shape[0]
    ways = lax.axis_size("expert")
    rows, chips = tok * ways, ways // 2
    dma = pltpu.SemaphoreType.DMA
    hbm = pl.BlockSpec(memory_space=pl.ANY)
    return pl.pallas_call(
        functools.partial(gather_kernel, homes, tok, 256),
        out_shape=[
            jax.ShapeDtypeStruct((2, rows, width), BF16),
            jax.ShapeDtypeStruct((3 * homes, rows, units), BF16),
        ],
        in_specs=[hbm] * 6,
        out_specs=[hbm] * 2,
        scratch_shapes=[
            pltpu.VMEM((2, rows, width), BF16),
            pltpu.VMEM((ways,) + mix.shape, F32),
            pltpu.VMEM(gate_matrix.shape, BF16),
            pltpu.VMEM(up_matrix.shape, BF16),
            pltpu.VMEM(down_matrix.shape, BF16),
            pltpu.VMEM((3 * homes, rows, units), BF16),
            dma((6,)),
            dma((2, chips)),
            dma((2, chips)),
            dma((2, chips)),
            dma((2, chips)),
            dma((2, chips)),
            dma((2, chips)),
        ],
        compiler_params=pltpu.CompilerParams(
            collective_id=1, has_side_effects=True, vmem_limit_bytes=56 * MIB
        ),
        cost_estimate=pl.CostEstimate(
            flops=2 * rows * width * units * 3 * homes, bytes_accessed=40 * MIB, transcendentals=0
        ),
    )(tokens, cotangent, mix, gate_matrix, up_matrix, down_matrix)


def outputs_kernel(homes, fac, gate, up, down, out, back):
    acc = dot(fac[2 * homes], down[0], 1, 0)
    for e in range(1, homes):
        acc += dot(fac[2 * homes + e], down[e], 1, 0)
    out[...] = acc.astype(BF16)
    acc = dot(fac[0], gate[0], 1, 1) + dot(fac[homes], up[0], 1, 1)
    for e in range(1, homes):
        acc += dot(fac[e], gate[e], 1, 1) + dot(fac[homes + e], up[e], 1, 1)
    back[...] = acc.astype(BF16)


def outputs_call(factors, gate_matrix, up_matrix, down_matrix):
    homes, width, units = gate_matrix.shape
    rows = factors.shape[1]
    tile = 256
    by_row = pl.BlockSpec((homes, tile, units), lambda i: (0, i, 0))
    by_col = pl.BlockSpec((homes, units, tile), lambda i: (0, 0, i))
    return pl.pallas_call(
        functools.partial(outputs_kernel, homes),
        grid=(width // tile,),
        out_shape=[jax.ShapeDtypeStruct((rows, width), BF16)] * 2,
        in_specs=[pl.BlockSpec(factors.shape, lambda i: (0, 0, 0)), by_row, by_row, by_col],
        out_specs=[pl.BlockSpec((rows, tile), lambda i: (0, i))] * 2,
        compiler_params=pltpu.CompilerParams(vmem_limit_bytes=56 * MIB),
        cost_estimate=pl.CostEstimate(
            flops=2 * rows * units * width * 3 * homes, bytes_accessed=36 * MIB, transcendentals=0
        ),
    )(factors, gate_matrix, up_matrix, down_matrix)


def grads_kernel(count, cols, both_hbm, factor_hbm, *refs):
    (out, both, factor, turned, stage, relay, land, in_sem, send_sem, relay_sem, land_sem) = refs
    split = 2 * count // 3
    me = lax.axis_index("dp")
    near_a = me + 1 - 2 * (me % 2)
    near_b = me + 2 - 4 * (me // 2)
    far = 3 - me

    loads = [
        pltpu.make_async_copy(both_hbm, both, in_sem.at[0]),
        pltpu.make_async_copy(factor_hbm, factor, in_sem.at[1]),
    ]
    for load in loads:
        load.start()
    barrier = pltpu.get_barrier_semaphore()
    for peer in (near_a, near_b):
        pl.semaphore_signal(
            barrier, inc=1, device_id={"dp": peer}, device_id_type=pl.DeviceIdType.MESH
        )
    pl.semaphore_wait(barrier, 2)
    for load in loads:
        load.wait()

    def remote(src, dst, send, recv, peer):
        return pltpu.make_async_remote_copy(
            src_ref=src,
            dst_ref=dst,
            send_sem=send,
            recv_sem=recv,
            device_id={"dp": peer},
            device_id_type=pl.DeviceIdType.MESH,
        )

    def to_relay(j, peer):
        return remote(stage.at[0, j], relay.at[j], send_sem.at[0, j], relay_sem.at[j], peer)

    def to_land(way, j, peer):
        return remote(
            stage.at[1 + way, j], land.at[way, j], send_sem.at[1 + way, j], land_sem.at[way, j], peer
        )

    def turn(owner):
        start = pl.multiple_of(owner * cols, cols)
        for side in range(2):
            turned[side] = both[side, :, pl.ds(start, cols)].T

    def chunk(j):
        return dot(turned[j // split], factor[j], 1, 0).astype(BF16)

    pairs = count // 2
    turn(far)

    @pl.loop(0, pairs)
    def _(k):
        for side, peer in ((0, near_a), (1, near_b)):
            j = 2 * k + side
            stage[0, j] = chunk(j)
            to_relay(j, peer).start()

    for way, peer in ((0, near_a), (1, near_b)):
        turn(peer)

        @pl.loop(0, pairs)
        def _(k, way=way, peer=peer):
            j = 2 * k + way
            stage[1 + way, j] = chunk(j)
            to_land(way, j, peer).start()
            other = 2 * k + 1 - way
            stage[1 + way, other] = chunk(other)

    turn(me)

    @pl.loop(0, count)
    def _(j):
        out[j] = chunk(j)

    @pl.loop(0, pairs)
    def _(k):
        for side, peer in ((0, near_a), (1, near_b)):
            j, way = 2 * k + side, 1 - side
            to_relay(j, peer).wait_recv()
            stage[1 + way, j] = (stage[1 + way, j].astype(F32) + relay[j].astype(F32)).astype(BF16)
            to_land(way, j, near_b if way else near_a).start()

    @pl.loop(0, count)
    def _(j):
        to_land(0, j, near_a).wait_recv()
        to_land(1, j, near_b).wait_recv()
        total = out[j].astype(F32) + land[0, j].astype(F32) + land[1, j].astype(F32)
        out[j] = total.astype(BF16)

    @pl.loop(0, count)
    def _(j):
        to_relay(j, near_a).wait_send()
        to_land(0, j, near_a).wait_send()
        to_land(1, j, near_b).wait_send()


def grads_call(both, factors):
    rows, width = both.shape[1:]
    count, _, units = factors.shape
    cols = width // lax.axis_size("dp")
    piece = (cols, units)
    dma = pltpu.SemaphoreType.DMA
    return pl.pallas_call(
        functools.partial(grads_kernel, count, cols),
        out_shape=jax.ShapeDtypeStruct((count,) + piece, BF16),
        in_specs=[pl.BlockSpec(memory_space=pl.ANY)] * 2,
        out_specs=pl.BlockSpec(memory_space=pltpu.VMEM),
        scratch_shapes=[
            pltpu.VMEM((2, rows, width), BF16),
            pltpu.VMEM((count, rows, units), BF16),
            pltpu.VMEM((2, cols, rows), BF16),
            pltpu.VMEM((3, count) + piece, BF16),
            pltpu.VMEM((count,) + piece, BF16),
            pltpu.VMEM((2, count) + piece, BF16),
            dma((2,)),
            dma((3, count)),
            dma((count,)),
            dma((2, count)),
        ],
        compiler_params=pltpu.CompilerParams(
            collective_id=0, has_side_effects=True, vmem_limit_bytes=60 * MIB
        ),
        cost_estimate=pl.CostEstimate(
            flops=2 * rows * width * units * count * 8, bytes_accessed=24 * MIB, transcendentals=0
        ),
    )(both, factors)


def with_kernels(tokens, routes, route_gates, gate_matrix, up_matrix, down_matrix, cotangent):
    homes = gate_matrix.shape[0]
    experts = jnp.arange(homes * lax.axis_size("expert"), dtype=jnp.int32)
    named = routes[None] == experts[:, None, None]
    mix = jnp.sum(jnp.where(named, route_gates[None], 0.0), axis=2)[:, None, :]
    both, factors = gather_call(tokens, cotangent, mix, gate_matrix, up_matrix, down_matrix)
    out, back = outputs_call(factors, gate_matrix, up_matrix, down_matrix)
    both, factors, out, back = lax.optimization_barrier((both, factors, out, back))
    summed = grads_call(both, factors)
    layer_out = lax.psum_scatter(out, "expert", scatter_dimension=0, tiled=True)
    grad_tokens = lax.psum_scatter(back, "expert", scatter_dimension=0, tiled=True)
    grad_gate, grad_up = summed[:homes], summed[homes : 2 * homes]
    grad_down = jnp.swapaxes(summed[2 * homes :], 1, 2)
    return (layer_out, grad_tokens, grad_gate, grad_up, grad_down)


def per_device(tokens, routes, route_gates, gate_matrix, up_matrix, down_matrix, cotangent):
    homes, width, units = gate_matrix.shape
    rows = tokens.shape[0] * lax.axis_size("expert")
    fits = rows * (2 * width + 3 * homes * units) * 2 <= 18 * MIB
    if fits and lax.axis_size("dp") == 4 and tokens.shape[0] == 128:
        return with_kernels(
            tokens, routes, route_gates, gate_matrix, up_matrix, down_matrix, cotangent
        )
    first = lax.axis_index("expert") * homes
    all_tokens = lax.all_gather(tokens, "expert", axis=0, tiled=True)
    all_cot = lax.all_gather(cotangent, "expert", axis=0, tiled=True)
    all_routes = lax.all_gather(routes, "expert", axis=0, tiled=True)
    all_gates = lax.all_gather(route_gates, "expert", axis=0, tiled=True)

    hidden, gpgs, gpus = [], [], []
    for e in range(homes):
        weight = jnp.sum(jnp.where(all_routes == first + e, all_gates, 0.0), axis=1, keepdims=True)
        pre_gate = dot(all_tokens, gate_matrix[e], 1, 0)
        pre_up = dot(all_tokens, up_matrix[e], 1, 0)
        grad_hidden = dot(all_cot, down_matrix[e], 1, 1) * weight
        s = jax.nn.sigmoid(pre_gate)
        act = pre_gate * s
        hidden.append((weight * act * pre_up).astype(BF16))
        gpgs.append((grad_hidden * pre_up * s * (1.0 + pre_gate * (1.0 - s))).astype(BF16))
        gpus.append((grad_hidden * act).astype(BF16))
    part_gate = jnp.stack([dot(all_tokens, g, 0, 0).astype(BF16) for g in gpgs])
    part_up = jnp.stack([dot(all_tokens, g, 0, 0).astype(BF16) for g in gpus])
    part_down = jnp.stack([dot(h, all_cot, 0, 0).astype(BF16) for h in hidden])
    grad_gate = lax.psum_scatter(part_gate, "dp", scatter_dimension=1, tiled=True)
    grad_up = lax.psum_scatter(part_up, "dp", scatter_dimension=1, tiled=True)
    grad_down = lax.psum_scatter(part_down, "dp", scatter_dimension=2, tiled=True)
    out = sum(dot(h, down_matrix[e], 1, 0) for e, h in enumerate(hidden)).astype(BF16)
    back = sum(
        dot(gpgs[e], gate_matrix[e], 1, 1) + dot(gpus[e], up_matrix[e], 1, 1)
        for e in range(homes)
    ).astype(BF16)
    layer_out = lax.psum_scatter(out, "expert", scatter_dimension=0, tiled=True)
    grad_tokens = lax.psum_scatter(back, "expert", scatter_dimension=0, tiled=True)
    return (layer_out, grad_tokens, grad_gate, grad_up, grad_down)


def solution(mesh):
    row = P(("dp", "expert"), None)
    home = P("expert", None, None)
    return jax.shard_map(
        per_device,
        mesh=mesh,
        in_specs=(row, row, row, home, home, home, row),
        out_specs=(row, row, P("expert", "dp", None), P("expert", "dp", None), P("expert", None, "dp")),
        check_vma=False,
    )
```

```python
import functools

import jax
import jax.numpy as jnp
from jax import lax
from jax.experimental import pallas as pl
from jax.experimental.pallas import tpu as pltpu
from jax.sharding import PartitionSpec as P

F32 = jnp.float32
BF16 = jnp.bfloat16
MIB = 1 << 20


def dot(a, b, ca, cb):
    return lax.dot_general(a, b, (((ca,), (cb,)), ((), ())), preferred_element_type=F32)


def gather_kernel(homes, tok, tile, tok_hbm, cot_hbm, mix_hbm, gate_hbm, up_hbm, down_hbm, *refs):
    (xc_out, fac_out, sum_out, sum_back, xc, mix, gate, up, down, fac, sums) = refs[:11]
    in_sem, out_sem, line_recv, core_recv, up_send, down_send, core_send = refs[11:]
    units = gate.shape[2]
    tiles = units // tile
    me = lax.axis_index("expert")
    chips = lax.axis_size("expert") // 2
    q, core = me // 2, me % 2
    partner = me + 1 - 2 * core
    first = me * homes

    def rows_of(b, count):
        return pl.ds(pl.multiple_of(b * tok, tok), count * tok)

    own = [
        pltpu.make_async_copy(tok_hbm, xc.at[0, rows_of(me, 1)], in_sem.at[0]),
        pltpu.make_async_copy(cot_hbm, xc.at[1, rows_of(me, 1)], in_sem.at[1]),
        pltpu.make_async_copy(mix_hbm, mix.at[me], in_sem.at[2]),
    ]
    weights = [
        pltpu.make_async_copy(gate_hbm, gate, in_sem.at[3]),
        pltpu.make_async_copy(up_hbm, up, in_sem.at[4]),
        pltpu.make_async_copy(down_hbm, down, in_sem.at[5]),
    ]
    for load in own + weights:
        load.start()

    barrier = pltpu.get_barrier_semaphore()

    def greet(peer):
        pl.semaphore_signal(
            barrier, inc=1, device_id={"expert": peer}, device_id_type=pl.DeviceIdType.MESH
        )

    greet(partner)

    @pl.when(q > 0)
    def _():
        greet(me - 2)

    @pl.when(q < chips - 1)
    def _():
        greet(me + 2)

    pl.semaphore_wait(barrier, jnp.where((q > 0) & (q < chips - 1), 3, 2))
    for load in own:
        load.wait()

    def moves(p, side, send, recv, peer):
        b = 2 * p + side
        return [
            pltpu.make_async_remote_copy(
                src_ref=ref,
                dst_ref=ref,
                send_sem=send.at[kind, p],
                recv_sem=recv.at[kind, p],
                device_id={"expert": peer},
                device_id_type=pl.DeviceIdType.MESH,
            )
            for kind, ref in enumerate((mix.at[b], xc.at[:, rows_of(b, 1), :]))
        ]

    def go_up(p):
        return moves(p, core, up_send, line_recv, me + 2)

    def go_down(p):
        return moves(p, core, down_send, line_recv, me - 2)

    def go_core(p):
        return moves(p, core, core_send, core_recv, partner)

    def start(copies):
        for copy in copies:
            copy.start()

    @pl.when(q < chips - 1)
    def _():
        start(go_up(q))

    @pl.when(q > 0)
    def _():
        start(go_down(q))

    start(go_core(q))
    for load in weights:
        load.wait()

    def stored(p):
        rows = rows_of(2 * p, 2)
        return [
            pltpu.make_async_copy(fac.at[:, rows, :], fac_out.at[:, rows, :], out_sem.at[0, p]),
            pltpu.make_async_copy(xc.at[:, rows, :], xc_out.at[:, rows, :], out_sem.at[1, p]),
            pltpu.make_async_copy(sums.at[0, rows, :], sum_out.at[rows, :], out_sem.at[2, p]),
            pltpu.make_async_copy(sums.at[1, rows, :], sum_back.at[rows, :], out_sem.at[3, p]),
        ]

    def compute(p):
        rows = rows_of(2 * p, 2)

        @pl.loop(0, homes * tiles)
        def _(i):
            e = i // tiles
            part = pl.ds(pl.multiple_of((i % tiles) * tile, tile), tile)
            weight = jnp.concatenate(
                [
                    jnp.broadcast_to(mix[2 * p + side, first + e], (128, tok)).T[:, :1]
                    for side in range(2)
                ],
                axis=0,
            )
            pre_gate = dot(xc[0, rows, :], gate[e, :, part], 1, 0)
            pre_up = dot(xc[0, rows, :], up[e, :, part], 1, 0)
            grad_hidden = dot(xc[1, rows, :], down[e, part, :], 1, 1) * weight
            s = jax.nn.sigmoid(pre_gate)
            act = pre_gate * s
            gpg = grad_hidden * pre_up * s * (1.0 + pre_gate * (1.0 - s))
            fac[e, rows, part] = gpg.astype(BF16)
            fac[homes + e, rows, part] = (grad_hidden * act).astype(BF16)
            fac[2 * homes + e, rows, part] = (weight * act * pre_up).astype(BF16)

        @pl.loop(0, gate.shape[1] // tile)
        def _(i):
            part = pl.ds(pl.multiple_of(i * tile, tile), tile)
            out = dot(fac[2 * homes, rows, :], down[0, :, part], 1, 0)
            back = dot(fac[0, rows, :], gate[0, part, :], 1, 1)
            back += dot(fac[homes, rows, :], up[0, part, :], 1, 1)
            for e in range(1, homes):
                out += dot(fac[2 * homes + e, rows, :], down[e, :, part], 1, 0)
                back += dot(fac[e, rows, :], gate[e, part, :], 1, 1)
                back += dot(fac[homes + e, rows, :], up[e, part, :], 1, 1)
            sums[0, rows, part] = out.astype(BF16)
            sums[1, rows, part] = back.astype(BF16)

        start(stored(p))

    @pl.loop(0, chips)
    def _(s):
        below, above = q - s, q + s

        @pl.when((s > 0) & (below >= 0))
        def _():
            for copy in moves(below, core, up_send, line_recv, me - 2):
                copy.wait_recv()

            @pl.when(q < chips - 1)
            def _():
                start(go_up(below))

            start(go_core(below))

        @pl.when((s > 0) & (above < chips))
        def _():
            for copy in moves(above, core, down_send, line_recv, me + 2):
                copy.wait_recv()

            @pl.when(q > 0)
            def _():
                start(go_down(above))

            start(go_core(above))

        @pl.loop(0, 2)
        def _(side):
            p = q + (2 * side - 1) * s

            @pl.when((s >= side) & (p >= 0) & (p < chips))
            def _():
                for copy in moves(p, 1 - core, core_send, core_recv, partner):
                    copy.wait_recv()
                compute(p)

    @pl.loop(0, chips)
    def _(p):
        for copy in stored(p):
            copy.wait()
        for copy in go_core(p):
            copy.wait_send()

        @pl.when((p <= q) & (q < chips - 1))
        def _():
            for copy in go_up(p):
                copy.wait_send()

        @pl.when((p >= q) & (q > 0))
        def _():
            for copy in go_down(p):
                copy.wait_send()


def gather_call(tokens, cotangent, mix, gate_matrix, up_matrix, down_matrix):
    homes, width, units = gate_matrix.shape
    tok = tokens.shape[0]
    ways = lax.axis_size("expert")
    rows, chips = tok * ways, ways // 2
    dma = pltpu.SemaphoreType.DMA
    hbm = pl.BlockSpec(memory_space=pl.ANY)
    return pl.pallas_call(
        functools.partial(gather_kernel, homes, tok, 256),
        out_shape=[
            jax.ShapeDtypeStruct((2, rows, width), BF16),
            jax.ShapeDtypeStruct((3 * homes, rows, units), BF16),
            jax.ShapeDtypeStruct((rows, width), BF16),
            jax.ShapeDtypeStruct((rows, width), BF16),
        ],
        in_specs=[hbm] * 6,
        out_specs=[hbm] * 4,
        scratch_shapes=[
            pltpu.VMEM((2, rows, width), BF16),
            pltpu.VMEM((ways,) + mix.shape, F32),
            pltpu.VMEM(gate_matrix.shape, BF16),
            pltpu.VMEM(up_matrix.shape, BF16),
            pltpu.VMEM(down_matrix.shape, BF16),
            pltpu.VMEM((3 * homes, rows, units), BF16),
            pltpu.VMEM((2, rows, width), BF16),
            dma((6,)),
            dma((4, chips)),
            dma((2, chips)),
            dma((2, chips)),
            dma((2, chips)),
            dma((2, chips)),
            dma((2, chips)),
        ],
        compiler_params=pltpu.CompilerParams(
            collective_id=1, has_side_effects=True, vmem_limit_bytes=60 * MIB
        ),
        cost_estimate=pl.CostEstimate(
            flops=2 * rows * width * units * 6 * homes, bytes_accessed=56 * MIB, transcendentals=0
        ),
    )(tokens, cotangent, mix, gate_matrix, up_matrix, down_matrix)


def grads_kernel(count, cols, both_hbm, factor_hbm, *refs):
    (out, both, factor, turned, stage, relay, land, in_sem, send_sem, relay_sem, land_sem) = refs
    split = 2 * count // 3
    me = lax.axis_index("dp")
    near_a = me + 1 - 2 * (me % 2)
    near_b = me + 2 - 4 * (me // 2)
    far = 3 - me

    loads = [
        pltpu.make_async_copy(both_hbm, both, in_sem.at[0]),
        pltpu.make_async_copy(factor_hbm, factor, in_sem.at[1]),
    ]
    for load in loads:
        load.start()
    barrier = pltpu.get_barrier_semaphore()
    for peer in (near_a, near_b):
        pl.semaphore_signal(
            barrier, inc=1, device_id={"dp": peer}, device_id_type=pl.DeviceIdType.MESH
        )
    pl.semaphore_wait(barrier, 2)
    for load in loads:
        load.wait()

    def remote(src, dst, send, recv, peer):
        return pltpu.make_async_remote_copy(
            src_ref=src,
            dst_ref=dst,
            send_sem=send,
            recv_sem=recv,
            device_id={"dp": peer},
            device_id_type=pl.DeviceIdType.MESH,
        )

    def to_relay(j, peer):
        return remote(stage.at[0, j], relay.at[j], send_sem.at[0, j], relay_sem.at[j], peer)

    def to_land(way, j, peer):
        return remote(
            stage.at[1 + way, j], land.at[way, j], send_sem.at[1 + way, j], land_sem.at[way, j], peer
        )

    def turn(owner):
        start = pl.multiple_of(owner * cols, cols)
        for side in range(2):
            turned[side] = both[side, :, pl.ds(start, cols)].T

    def chunk(j):
        return dot(turned[j // split], factor[j], 1, 0).astype(BF16)

    pairs = count // 2
    turn(far)

    @pl.loop(0, pairs)
    def _(k):
        for side, peer in ((0, near_a), (1, near_b)):
            j = 2 * k + side
            stage[0, j] = chunk(j)
            to_relay(j, peer).start()

    for way, peer in ((0, near_a), (1, near_b)):
        turn(peer)

        @pl.loop(0, pairs)
        def _(k, way=way, peer=peer):
            j = 2 * k + way
            stage[1 + way, j] = chunk(j)
            to_land(way, j, peer).start()
            other = 2 * k + 1 - way
            stage[1 + way, other] = chunk(other)

    turn(me)

    @pl.loop(0, count)
    def _(j):
        out[j] = chunk(j)

    @pl.loop(0, pairs)
    def _(k):
        for side, peer in ((0, near_a), (1, near_b)):
            j, way = 2 * k + side, 1 - side
            to_relay(j, peer).wait_recv()
            stage[1 + way, j] = (stage[1 + way, j].astype(F32) + relay[j].astype(F32)).astype(BF16)
            to_land(way, j, near_b if way else near_a).start()

    @pl.loop(0, count)
    def _(j):
        to_land(0, j, near_a).wait_recv()
        to_land(1, j, near_b).wait_recv()
        total = out[j].astype(F32) + land[0, j].astype(F32) + land[1, j].astype(F32)
        out[j] = total.astype(BF16)

    @pl.loop(0, count)
    def _(j):
        to_relay(j, near_a).wait_send()
        to_land(0, j, near_a).wait_send()
        to_land(1, j, near_b).wait_send()


def grads_call(both, factors):
    rows, width = both.shape[1:]
    count, _, units = factors.shape
    cols = width // lax.axis_size("dp")
    piece = (cols, units)
    dma = pltpu.SemaphoreType.DMA
    return pl.pallas_call(
        functools.partial(grads_kernel, count, cols),
        out_shape=jax.ShapeDtypeStruct((count,) + piece, BF16),
        in_specs=[pl.BlockSpec(memory_space=pl.ANY)] * 2,
        out_specs=pl.BlockSpec(memory_space=pltpu.VMEM),
        scratch_shapes=[
            pltpu.VMEM((2, rows, width), BF16),
            pltpu.VMEM((count, rows, units), BF16),
            pltpu.VMEM((2, cols, rows), BF16),
            pltpu.VMEM((3, count) + piece, BF16),
            pltpu.VMEM((count,) + piece, BF16),
            pltpu.VMEM((2, count) + piece, BF16),
            dma((2,)),
            dma((3, count)),
            dma((count,)),
            dma((2, count)),
        ],
        compiler_params=pltpu.CompilerParams(
            collective_id=0, has_side_effects=True, vmem_limit_bytes=60 * MIB
        ),
        cost_estimate=pl.CostEstimate(
            flops=2 * rows * width * units * count * 8, bytes_accessed=24 * MIB, transcendentals=0
        ),
    )(both, factors)


def with_kernels(tokens, routes, route_gates, gate_matrix, up_matrix, down_matrix, cotangent):
    homes = gate_matrix.shape[0]
    experts = jnp.arange(homes * lax.axis_size("expert"), dtype=jnp.int32)
    named = routes[None] == experts[:, None, None]
    mix = jnp.sum(jnp.where(named, route_gates[None], 0.0), axis=2)[:, None, :]
    both, factors, out, back = gather_call(
        tokens, cotangent, mix, gate_matrix, up_matrix, down_matrix
    )
    both, factors, out, back = lax.optimization_barrier((both, factors, out, back))
    summed = grads_call(both, factors)
    layer_out = lax.psum_scatter(out, "expert", scatter_dimension=0, tiled=True)
    grad_tokens = lax.psum_scatter(back, "expert", scatter_dimension=0, tiled=True)
    grad_gate, grad_up = summed[:homes], summed[homes : 2 * homes]
    grad_down = jnp.swapaxes(summed[2 * homes :], 1, 2)
    return (layer_out, grad_tokens, grad_gate, grad_up, grad_down)


def per_device(tokens, routes, route_gates, gate_matrix, up_matrix, down_matrix, cotangent):
    homes, width, units = gate_matrix.shape
    rows = tokens.shape[0] * lax.axis_size("expert")
    fits = rows * (2 * width + 3 * homes * units) * 2 <= 18 * MIB
    if fits and lax.axis_size("dp") == 4 and tokens.shape[0] == 128:
        return with_kernels(
            tokens, routes, route_gates, gate_matrix, up_matrix, down_matrix, cotangent
        )
    first = lax.axis_index("expert") * homes
    all_tokens = lax.all_gather(tokens, "expert", axis=0, tiled=True)
    all_cot = lax.all_gather(cotangent, "expert", axis=0, tiled=True)
    all_routes = lax.all_gather(routes, "expert", axis=0, tiled=True)
    all_gates = lax.all_gather(route_gates, "expert", axis=0, tiled=True)

    hidden, gpgs, gpus = [], [], []
    for e in range(homes):
        weight = jnp.sum(jnp.where(all_routes == first + e, all_gates, 0.0), axis=1, keepdims=True)
        pre_gate = dot(all_tokens, gate_matrix[e], 1, 0)
        pre_up = dot(all_tokens, up_matrix[e], 1, 0)
        grad_hidden = dot(all_cot, down_matrix[e], 1, 1) * weight
        s = jax.nn.sigmoid(pre_gate)
        act = pre_gate * s
        hidden.append((weight * act * pre_up).astype(BF16))
        gpgs.append((grad_hidden * pre_up * s * (1.0 + pre_gate * (1.0 - s))).astype(BF16))
        gpus.append((grad_hidden * act).astype(BF16))
    part_gate = jnp.stack([dot(all_tokens, g, 0, 0).astype(BF16) for g in gpgs])
    part_up = jnp.stack([dot(all_tokens, g, 0, 0).astype(BF16) for g in gpus])
    part_down = jnp.stack([dot(h, all_cot, 0, 0).astype(BF16) for h in hidden])
    grad_gate = lax.psum_scatter(part_gate, "dp", scatter_dimension=1, tiled=True)
    grad_up = lax.psum_scatter(part_up, "dp", scatter_dimension=1, tiled=True)
    grad_down = lax.psum_scatter(part_down, "dp", scatter_dimension=2, tiled=True)
    out = sum(dot(h, down_matrix[e], 1, 0) for e, h in enumerate(hidden)).astype(BF16)
    back = sum(
        dot(gpgs[e], gate_matrix[e], 1, 1) + dot(gpus[e], up_matrix[e], 1, 1)
        for e in range(homes)
    ).astype(BF16)
    layer_out = lax.psum_scatter(out, "expert", scatter_dimension=0, tiled=True)
    grad_tokens = lax.psum_scatter(back, "expert", scatter_dimension=0, tiled=True)
    return (layer_out, grad_tokens, grad_gate, grad_up, grad_down)


def solution(mesh):
    row = P(("dp", "expert"), None)
    home = P("expert", None, None)
    return jax.shard_map(
        per_device,
        mesh=mesh,
        in_specs=(row, row, row, home, home, home, row),
        out_specs=(row, row, P("expert", "dp", None), P("expert", "dp", None), P("expert", None, "dp")),
        check_vma=False,
    )
```
